256 devices in a mesh: dp: 32 (over z_hi, y, core), tensor: 8 (over x, z_lo).
Axes of the slice: x: 4, y: 4, z: 8 (z_hi: 4, z_lo: 2; z = z_hi * 2 + z_lo), core: 2. Of those that a mesh axis runs over, the one named last changes fastest.
Arguments:
- gate_pre: bfloat16 [8192, 14336], P('dp', 'tensor'), may hold values from -6 to 6
- up_pre: bfloat16 [8192, 14336], P('dp', 'tensor'), may hold values from -6 to 6
- cotangent: bfloat16 [8192, 4096], P(('dp', 'tensor')), may hold values from -24 to 24
- w_prev: bfloat16 [14336, 4096], P('tensor', 'dp'), may hold values from -0.09375 to 0.09375
- param_next: float32 [14336, 4096], P('tensor', 'dp'), may hold values from -0.75 to 0.75
- grad_next: float32 [14336, 4096], P('tensor', 'dp'), may hold values from -6 to 6
- moment_one: bfloat16 [14336, 4096], P('tensor', 'dp'), may hold values from -4 to 4
- moment_two: bfloat16 [14336, 4096], P('tensor', 'dp'), may hold values from 0.0099487305 to 1
Outputs:
- gate_grad: bfloat16 [8192, 14336], P('dp', 'tensor')
- up_grad: bfloat16 [8192, 14336], P('dp', 'tensor')
- grad_prev: float32 [14336, 4096], P('tensor', 'dp')
- param_new: float32 [14336, 4096], P('tensor', 'dp')
- moment_one_new: bfloat16 [14336, 4096], P('tensor', 'dp')
- moment_two_new: bfloat16 [14336, 4096], P('tensor', 'dp')
- adam_step: float32 [14336, 4096], P('tensor', 'dp')
The draws below stay inside these ranges and needn't reach their ends.
All inputs are finite; a program needn't handle non-finite values.
Results may differ from the reference program's by a relative error of at most 0.02.
Values may be sent and summed in bfloat16 or wider, within the bound.
A program may use at most 128 MiB of HBM per device.

```python
import math
import jax
import jax.numpy as jnp
from jax import lax

D = 4096
FF_W = 14336
TOK_DEV = 256
STEP = 10
TOKENS = 8192
N_DP = 32


def strengthened(entries, key, source, target, parts, factor):
    owner, partner = [(jnp.arange(entries.shape[position]) // (entries.shape[position] // parts)).reshape([-1 if axis == position else 1 for axis in range(entries.ndim)]) for position in (source, target)]
    chosen = jax.random.permutation(key, parts)[partner]
    strong = (owner == chosen) | (owner == (partner + parts // 2) % parts)
    return jnp.where(strong, factor * entries, entries)


def steps_of(key, dims, split, smallest, high):
    loudness = 1.0
    for position, shards_of in split:
        steps = jax.random.uniform(jax.random.fold_in(jax.random.fold_in(key, 6), position), (shards_of,), jnp.float32, smallest / len(split), high / len(split))
        loudness = loudness * jnp.repeat(jnp.exp(steps), dims[position] // shards_of).reshape((-1,) + (1,) * (len(dims) - 1 - position))
    return loudness


def scatter_about(key, dims, width, limit, split=(), held_as=jnp.bfloat16):
    level = steps_of(key, dims, split, -0.22, 0.18) if split else 1.0
    result = jax.random.normal(key, dims, jnp.float32) * width * level
    return jnp.minimum(jnp.maximum(result, -limit), limit).astype(held_as)


def bell_draw_with(stream_key, shape, scale, most, pieces, heavy, dtype=jnp.bfloat16):
    array = scale * jax.random.normal(stream_key, shape, jnp.float32)
    if pieces:
        array = array * steps_of(stream_key, shape, pieces, -0.22, 0.18)
    return jnp.clip(strengthened(array, jax.random.fold_in(stream_key, 3), *heavy), -most, most).astype(dtype)


def setup_inputs(seed: int = 0) -> dict:
    key_list = jax.random.split(jax.random.key(seed), 9)
    return {
        "gate_pre": scatter_about(key_list[0], (TOKENS, FF_W), 1.0, 6.0, ((0, 32), (1, 8))),
        "up_pre": scatter_about(key_list[1], (TOKENS, FF_W), 1.0, 6.0, ((0, 32), (1, 8))),
        "cotangent": bell_draw_with(key_list[2], (TOKENS, D), 1.0, 24.0, ((0, 256),), (0, 1, 256, 6.0)),
        "w_prev": scatter_about(key_list[3], (FF_W, D), D ** -0.5, 0.09375, ((0, 8), (1, 32))),
        "param_next": scatter_about(key_list[4], (FF_W, D), 0.05, 0.75, ((0, 8), (1, 32)), jnp.float32),
        "grad_next": scatter_about(key_list[5], (FF_W, D), 1.0, 6.0, ((0, 8), (1, 32)), jnp.float32),
        "moment_one": scatter_about(key_list[6], (FF_W, D), 0.3, 4.0, ((0, 8), (1, 32))),
        "moment_two": jnp.clip(jnp.exp(math.log(1.0) - 4.61031033 * jax.random.uniform(key_list[7], (FF_W, D), jnp.float32) ** steps_of(key_list[7], (FF_W, D), ((0, 8), (1, 32)), -0.2, 0.2)), 0.0099487305, 1.0).astype(jnp.bfloat16),
    }


beta_first = 0.9
beta_second = 0.95
epsilon = 1e-08
decay_rate = 0.1
learn_rate = 0.0003
unscale = 1.0 / 32.0

def reference(gate_pre, up_pre, cotangent, w_prev, param_next, grad_next, moment_one, moment_two):
    gate_vals = gate_pre.astype(jnp.float32)
    up_vals = up_pre.astype(jnp.float32)
    gate_sig = jax.nn.sigmoid(gate_vals)
    gate_act = gate_vals * gate_sig
    hidden = (gate_act * up_vals).astype(jnp.bfloat16)
    hidden_grad = jnp.dot(cotangent, w_prev.T, preferred_element_type=jnp.float32)
    up_grad = (hidden_grad * gate_act).astype(jnp.bfloat16)
    gate_grad = (hidden_grad * up_vals * gate_sig * (1.0 + gate_vals * (1.0 - gate_sig))).astype(jnp.bfloat16)
    cot_groups = cotangent.reshape(N_DP, TOK_DEV, D)
    hid_groups = hidden.reshape(N_DP, TOK_DEV, FF_W)

    def accumulate(running, inputs):
        cot_block, hid_block = inputs
        group_term = lax.dot_general(cot_block, hid_block, (((0,), (0,)), ((), ())), preferred_element_type=jnp.float32)
        group_term = lax.optimization_barrier(group_term.astype(jnp.bfloat16)).astype(jnp.float32)
        return (running + group_term, None)
    summed, _ = lax.scan(accumulate, jnp.zeros((D, FF_W), jnp.float32), (cot_groups, hid_groups))
    grad_prev = (summed * unscale).T
    moment_one_f = beta_first * moment_one.astype(jnp.float32) + (1.0 - beta_first) * grad_next
    moment_two_f = beta_second * moment_two.astype(jnp.float32) + (1.0 - beta_second) * grad_next * grad_next
    first_fix = 1.0 - beta_first ** STEP
    second_fix = 1.0 - beta_second ** STEP
    adam_step = moment_one_f / first_fix / (jnp.sqrt(moment_two_f / second_fix) + epsilon) + decay_rate * param_next
    param_new = param_next - learn_rate * adam_step
    return (gate_grad, up_grad, grad_prev, param_new, moment_one_f.astype(jnp.bfloat16), moment_two_f.astype(jnp.bfloat16), adam_step)
```

```python
import jax
import jax.numpy as jnp
from jax import lax
from jax.experimental import pallas as pl
from jax.experimental.pallas import tpu as pltpu
from jax.sharding import PartitionSpec as P

STEP = 10


beta_first = 0.9
beta_second = 0.95
epsilon = 1e-08
decay_rate = 0.1
learn_rate = 0.0003
unscale = 1.0 / 32.0

MESH = pl.DeviceIdType.MESH
F32, BF16 = jnp.float32, jnp.bfloat16

TOK, HID, QUARTER, WIDE, CHUNK, SHARD = 256, 1792, 448, 512, 1024, 128
ORD = (2, 1, 3, 0)
SLOT = {o: k for k, o in enumerate(ORD)}
STEPS = [(k, j) for k in range(3) for j in (0, 1, 3, 2)] + [(3, j) for j in (2, 3, 1, 0)]
RIGHT = (0, 3)


def back(j):
    return (4 - j) % 4


def kernel(
    gate_ref, up_ref, cot_ref, w_ref, gg_ref, ug_ref, gp_ref,
    gate_v, up_v, act_v, fac_v, hidh, hidt, cot_v, w_v, px_s, px_r, pown, ps, gr,
    hg_acc, hg_s, hg_r, gg_v, ug_v, gp_v,
    ld, zl_s, zl_r, y_s, y_r, xr_s, xl_s, fl_r, fr_r, xf_s, xf_r, w_s, w_r, wc_s, wc_r,
    h_s, h_r, g_s, g_r, pc_s, pc_r, p_s, p_r, out_s,
):
    dp, tn = lax.axis_index("dp"), lax.axis_index("tensor")
    c, y, zh = dp % 2, (dp // 2) % 4, dp // 8
    x, zl = tn // 2, tn % 2

    def plane(o, j):
        return ((((zh + o) % 4) * 4 + (y + j) % 4) * 2 + c, tn)

    other_core = (dp + 1 - 2 * c, tn)
    other_zl = (dp, tn + 1 - 2 * zl)
    right = (dp, ((x + 1) % 4) * 2 + zl)
    left = (dp, ((x + 3) % 4) * 2 + zl)

    def remote(src, dst, send, recv, device):
        return pltpu.make_async_remote_copy(
            src_ref=src, dst_ref=dst, send_sem=send, recv_sem=recv,
            device_id=device, device_id_type=MESH,
        )

    sent = []

    def start(copy):
        copy.start()
        sent.append(copy)

    def arrived(ref, recv, send):
        remote(ref, ref, send, recv, other_core).wait_recv()

    def chunk_cols(k):
        return pl.ds(pl.multiple_of(((zh + ORD[k]) % 4) * CHUNK, CHUNK), CHUNK)

    def rows_at(j, xx, n=64, extra=0):
        return pl.ds(pl.multiple_of(j * TOK + xx * 64 + extra, 32), n)

    peers = [plane(o, j) for o in range(4) for j in range(4) if (o, j) != (0, 0)]
    peers += [other_core, other_zl, right, left]
    barrier = pltpu.get_barrier_semaphore()
    for peer in peers:
        pl.semaphore_signal(barrier, inc=1, device_id=peer, device_id_type=MESH)

    own_rows = rows_at(0, x, 32, zl * 32)
    loads = []
    for k in range(4):
        loads.append(pltpu.make_async_copy(
            cot_ref.at[:, chunk_cols(k)], cot_v.at[k, own_rows], ld.at[k]))
    loads.append(pltpu.make_async_copy(gate_ref, gate_v, ld.at[4]))
    loads.append(pltpu.make_async_copy(up_ref, up_v, ld.at[5]))

    def quarter_rows(j):
        return pl.ds(pl.multiple_of(((y + j) % 4) * QUARTER, QUARTER), QUARTER)

    def w_rows(j):
        return pl.ds(pl.multiple_of(((y + j) % 2) * 64, 64), QUARTER)

    def w_cols(j, cc):
        return pl.ds(pl.multiple_of((((y + j) % 4) * 2 + cc) * SHARD, SHARD), SHARD)

    loads.append(pltpu.make_async_copy(
        w_ref.at[quarter_rows(0)], w_v.at[3, w_rows(0), w_cols(0, c)], ld.at[6]))
    for load in loads:
        load.start()
    pad = pl.ds(pl.multiple_of((1 - y % 2) * QUARTER, 64), 64)
    for k in range(4):
        w_v[k, pad, :] = jnp.zeros((64, CHUNK), BF16)
    pl.semaphore_wait(barrier, len(peers))

    for k in range(4):
        start(remote(cot_ref.at[:, chunk_cols(k)], cot_v.at[k, own_rows],
                     zl_s.at[k], zl_r.at[k], other_zl))
    partner_rows = rows_at(0, x, 32, (1 - zl) * 32)

    def y_sends(k):
        loads[k].wait()
        arrived(cot_v.at[k, partner_rows], zl_r.at[k], zl_s.at[k])
        for j in ((2, 3, 1) if k == 3 else (1, 3, 2)):
            start(remote(cot_v.at[k, rows_at(0, x)], cot_v.at[k, rows_at(back(j), x)],
                         y_s.at[k, j], y_r.at[k, back(j)], plane(0, j)))

    def w_sends():
        for o, j in [(1, 0), (3, 0), (1, 1), (3, 1), (1, 3), (3, 3), (1, 2), (3, 2),
                     (0, 1), (0, 3), (0, 2)]:
            k = SLOT[back(o)]
            start(remote(w_ref.at[quarter_rows(j)], w_v.at[k, w_rows(j), w_cols(0, c)],
                         w_s.at[k, back(j)], w_r.at[k, back(j)], plane(o, j)))

    def w_block(k, j, cc):
        return w_v.at[k, w_rows(0), w_cols(j, cc)]

    def w_arrived(k, j):
        if (k, j) == (3, 0):
            loads[6].wait()
        else:
            arrived(w_block(k, j, c), w_r.at[k, j], w_s.at[k, j])
        start(remote(w_block(k, j, c), w_block(k, j, c), wc_s.at[k, j], wc_r.at[k, j], other_core))

    def w_near():
        for k, o, blocks in ((SLOT[1], 3, (0, 1)), (SLOT[3], 1, (2, 3))):
            for j in range(4):
                w_arrived(k, j)
                if j in blocks:
                    start(remote(w_block(k, j, c), w_block(0, j, c),
                                 w_s.at[0, j], w_r.at[0, j], plane(o, 0)))
        for j in range(4):
            w_arrived(3, j)

    def w_far():
        for j in range(4):
            w_arrived(0, j)

    def w_other(k):
        for j in range(4):
            arrived(w_block(k, j, 1 - c), wc_r.at[k, j], wc_s.at[k, j])

    def home():
        loads[4].wait()
        loads[5].wait()

        def block(f, _):
            cols = pl.ds(pl.multiple_of(f * 128, 128), 128)
            g = gate_v[:, cols].astype(F32)
            u = up_v[:, cols].astype(F32)
            s = jax.nn.sigmoid(g)
            act = g * s
            act_v[:, cols] = act
            fac_v[:, cols] = u * s * (1.0 + g * (1.0 - s))
            hidh[cols, :] = (act * u).T.astype(BF16)
            return 0

        lax.fori_loop(0, HID // 128, block, 0)

    def hidden_sends():
        for j in (2, 1, 3):
            start(remote(hidh.at[quarter_rows(j)], hidt.at[:, pl.ds(back(j) * TOK, TOK)],
                         h_s.at[j], h_r.at[back(j)], plane(0, j)))
        hidt[:, 0:TOK] = hidh[quarter_rows(0), :]

    def hidden_arrived():
        for j in (1, 3, 2):
            arrived(hidt.at[:, pl.ds(j * TOK, TOK)], h_r.at[j], h_s.at[j])

    def term(k):
        def tile(j, _):
            cols = pl.ds(pl.multiple_of(((y + j) % 4) * 256, 256), 256)
            part = jnp.dot(hidt[...], cot_v[k, :, cols], preferred_element_type=F32)
            low, high = part[:, :SHARD], part[:, SHARD:]
            pown[j] = jnp.where(c == 0, low, high)
            px_s[k, j] = jnp.where(c == 0, high, low).astype(BF16)
            return 0

        lax.fori_loop(0, 4, tile, 0)
        start(remote(px_s.at[k], px_r.at[k], pc_s.at[k], pc_r.at[k], other_core))

    def term_sends(k):
        arrived(px_r.at[k], pc_r.at[k], pc_s.at[k])
        for j in (2, 1, 3, 0):
            total = (pown[j] + px_r[k, j].astype(F32)).astype(BF16)
            if (k, j) == (3, 0):
                gr[3, 0] = total
            else:
                ps[k, j] = total
                start(remote(ps.at[k, j], gr.at[k, back(j)], p_s.at[k, j],
                             p_r.at[k, back(j)], plane(ORD[k], j)))

    def grad_part(k, j):
        rows = pl.ds(j * TOK, TOK) if isinstance(j, int) else pl.ds(pl.multiple_of(j * TOK, TOK), TOK)
        return lax.dot_general(cot_v[k, rows, :], w_v[k], (((1,), (1,)), ((), ())),
                               preferred_element_type=F32)

    def grad_add(k, first):
        def tile(j, _):
            part = grad_part(k, j)
            hg_acc[j] = part if first else hg_acc[j] + part
            return 0

        lax.fori_loop(0, 4, tile, 0)

    def grad_sends(j):
        hg_s[j] = (hg_acc[j] + grad_part(3, j)).astype(BF16)
        if j == 0:
            copy = pltpu.make_async_copy(hg_s.at[0], hg_r.at[y], g_r.at[y])
            copy.start()
        else:
            start(remote(hg_s.at[j], hg_r.at[y], g_s.at[j], g_r.at[y], plane(0, j)))

    y_sends(0)
    w_sends()
    home()
    hidden_sends()
    pending = []
    for i in range(len(STEPS) + 2):
        if i < len(STEPS):
            k, j = STEPS[i]
            if j:
                arrived(cot_v.at[k, rows_at(j, x)], y_r.at[k, j], y_s.at[k, j])
            mine = cot_v.at[k, rows_at(j, x)]
            start(remote(mine, mine, xr_s.at[k, j], fl_r.at[k, j], right))
            start(remote(mine, mine, xl_s.at[k, j], fr_r.at[k, j], left))
            if i in (0, 4, 8):
                y_sends(k + 1)
        if 1 <= i <= len(STEPS):
            k, j = STEPS[i - 1]
            from_left = cot_v.at[k, rows_at(j, (x + 3) % 4)]
            from_right = cot_v.at[k, rows_at(j, (x + 1) % 4)]
            arrived(from_left, fl_r.at[k, j], xr_s.at[k, j])
            arrived(from_right, fr_r.at[k, j], xl_s.at[k, j])
            block, device = (from_left, right) if j in RIGHT else (from_right, left)
            start(remote(block, block, xf_s.at[k, j], xf_r.at[k, j], device))
        for k in pending:
            term_sends(k)
        pending = []
        if i >= 2:
            k, j = STEPS[i - 2]
            arrived(cot_v.at[k, rows_at(j, (x + 2) % 4)], xf_r.at[k, j], xf_s.at[k, j])
            if i == 3:
                w_near()
            if i == 5:
                hidden_arrived()
            if i == 8:
                w_far()
            if k == 3:
                if j:
                    grad_sends(j)
            elif STEPS[i - 1][0] != k:
                term(k)
                pending.append(k)
                if k == 1:
                    w_other(1)
                    grad_add(1, True)
                if k == 2:
                    w_other(2)
                    grad_add(2, False)
                    w_other(0)
                    grad_add(0, False)
                    w_other(3)
    term(3)
    grad_sends(0)
    term_sends(3)

    for yy in range(4):
        arrived(hg_r.at[yy], g_r.at[yy], g_s.at[0])

    stores = []

    def result(r, _):
        rows = pl.ds(pl.multiple_of(r * 32, 32), 32)
        p = [hg_r[q, rows, :].astype(F32) for q in range(4)]
        grad = jnp.concatenate(
            [p[0][:, :384], p[0][:, 384:] + p[1][:, :128], p[1][:, 128:],
             p[2][:, :384], p[2][:, 384:] + p[3][:, :128], p[3][:, 128:]], axis=1)
        ug_v[rows, :] = (grad * act_v[rows, :]).astype(BF16)
        gg_v[rows, :] = (grad * fac_v[rows, :]).astype(BF16)
        return 0

    for half in range(2):
        lax.fori_loop(half * 4, half * 4 + 4, result, 0)
        rows = pl.ds(half * 128, 128)
        for n, (src, dst) in enumerate(((ug_v, ug_ref), (gg_v, gg_ref))):
            stores.append(pltpu.make_async_copy(src.at[rows], dst.at[rows], out_s.at[half * 2 + n]))
            stores[-1].start()
    for j in (0, 1, 3, 2):
        total = None
        for k in range(4):
            if (k, j) != (3, 0):
                arrived(gr.at[k, j], p_r.at[k, j], p_s.at[k, j])
            part = gr[k, j].astype(F32)
            total = part if total is None else total + part
        gp_v[quarter_rows(j), :] = total * unscale
        stores.append(pltpu.make_async_copy(
            gp_v.at[quarter_rows(j)], gp_ref.at[quarter_rows(j)], out_s.at[4 + j]))
        stores[-1].start()
    for copy in sent:
        copy.wait_send()
    for store in stores:
        store.wait()


def grads(gate_pre, up_pre, cotangent, w_prev):
    def dma(*shape):
        return pltpu.SemaphoreType.DMA(shape)

    any_spec = pl.BlockSpec(memory_space=pl.ANY)
    scratch = [
        pltpu.VMEM((TOK, HID), BF16),
        pltpu.VMEM((TOK, HID), BF16),
        pltpu.VMEM((TOK, HID), F32),
        pltpu.VMEM((TOK, HID), F32),
        pltpu.VMEM((HID, TOK), BF16),
        pltpu.VMEM((QUARTER, 4 * TOK), BF16),
        pltpu.VMEM((4, 4 * TOK, CHUNK), BF16),
        pltpu.VMEM((4, WIDE, CHUNK), BF16),
        pltpu.VMEM((4, 4, QUARTER, SHARD), BF16),
        pltpu.VMEM((4, 4, QUARTER, SHARD), BF16),
        pltpu.VMEM((4, QUARTER, SHARD), F32),
        pltpu.VMEM((4, 4, QUARTER, SHARD), BF16),
        pltpu.VMEM((4, 4, QUARTER, SHARD), BF16),
        pltpu.VMEM((4, TOK, WIDE), F32),
        pltpu.VMEM((4, TOK, WIDE), BF16),
        pltpu.VMEM((4, TOK, WIDE), BF16),
        pltpu.VMEM((TOK, HID), BF16),
        pltpu.VMEM((TOK, HID), BF16),
        pltpu.VMEM((HID, SHARD), F32),
        dma(8), dma(4), dma(4), dma(4, 4), dma(4, 4),
        dma(4, 4), dma(4, 4), dma(4, 4), dma(4, 4), dma(4, 4), dma(4, 4),
        dma(4, 4), dma(4, 4), dma(4, 4), dma(4, 4),
        dma(4), dma(4), dma(4), dma(4),
        dma(4), dma(4), dma(4, 4), dma(4, 4), dma(8),
    ]
    return pl.pallas_call(
        kernel,
        out_shape=(
            jax.ShapeDtypeStruct((TOK, HID), BF16),
            jax.ShapeDtypeStruct((TOK, HID), BF16),
            jax.ShapeDtypeStruct((HID, SHARD), F32),
        ),
        in_specs=[any_spec] * 4,
        out_specs=(any_spec,) * 3,
        scratch_shapes=scratch,
        compiler_params=pltpu.CompilerParams(
            collective_id=0, has_side_effects=True, vmem_limit_bytes=52 * 2**20
        ),
        cost_estimate=pl.CostEstimate(
            flops=4 * TOK * HID * 4096, bytes_accessed=8 * 2**20, transcendentals=TOK * HID
        ),
    )(gate_pre, up_pre, cotangent, w_prev)


def body(gate_pre, up_pre, cotangent, w_prev, param_next, grad_next, moment_one, moment_two):
    gate_grad, up_grad, grad_prev = grads(gate_pre, up_pre, cotangent, w_prev)
    moment_one_f = beta_first * moment_one.astype(jnp.float32) + (1.0 - beta_first) * grad_next
    moment_two_f = (
        beta_second * moment_two.astype(jnp.float32) + (1.0 - beta_second) * grad_next * grad_next
    )
    first_fix = 1.0 - beta_first**STEP
    second_fix = 1.0 - beta_second**STEP
    adam_step = (
        moment_one_f / first_fix / (jnp.sqrt(moment_two_f / second_fix) + epsilon)
        + decay_rate * param_next
    )
    param_new = param_next - learn_rate * adam_step
    return (
        gate_grad,
        up_grad,
        grad_prev,
        param_new,
        moment_one_f.astype(jnp.bfloat16),
        moment_two_f.astype(jnp.bfloat16),
        adam_step,
    )


def solution(mesh):
    in_specs = (
        P("dp", "tensor"),
        P("dp", "tensor"),
        P(("dp", "tensor"), None),
        P("tensor", "dp"),
        P("tensor", "dp"),
        P("tensor", "dp"),
        P("tensor", "dp"),
        P("tensor", "dp"),
    )
    out_specs = (
        P("dp", "tensor"),
        P("dp", "tensor"),
        P("tensor", "dp"),
        P("tensor", "dp"),
        P("tensor", "dp"),
        P("tensor", "dp"),
        P("tensor", "dp"),
    )
    return jax.shard_map(body, mesh=mesh, in_specs=in_specs, out_specs=out_specs, check_vma=False)
```

```python
import jax
import jax.numpy as jnp
from jax import lax
from jax.experimental import pallas as pl
from jax.experimental.pallas import tpu as pltpu
from jax.sharding import PartitionSpec as P

STEP = 10


beta_first = 0.9
beta_second = 0.95
epsilon = 1e-08
decay_rate = 0.1
learn_rate = 0.0003
unscale = 1.0 / 32.0

MESH = pl.DeviceIdType.MESH
F32, BF16 = jnp.float32, jnp.bfloat16

TOK, HID, QUARTER, WIDE, CHUNK, SHARD = 256, 1792, 448, 512, 1024, 128
ORD = (2, 1, 3, 0)
SLOT = {o: k for k, o in enumerate(ORD)}
RIGHT = (0, 3)
ORDER = (
    ("wsend",), ("ysend", 0), ("own", 0, 0), ("ysend", 1), ("own", 1, 0), ("farr",), ("ysend", 2),
    ("home", 0), ("wown", 1), ("own", 2, 0), ("wown", 2), ("own", 0, 3), ("own", 0, 2),
    ("home", 1), ("own", 1, 1), ("own", 0, 1), ("fwd", 0, 2), ("fwd", 0, 0), ("wown", 3),
    ("own", 1, 2), ("wnear", 2), ("home", 2), ("own", 1, 3), ("home", 3), ("fwd", 0, 3),
    ("hsend",), ("wnear", 1), ("fwd", 0, 1), ("wown", 0), ("done", 0, 0), ("fwd", 1, 2),
    ("done", 0, 2), ("wnear", 3), ("own", 2, 1), ("harr",), ("fwd", 1, 3), ("own", 2, 3),
    ("fwd", 1, 1), ("done", 0, 3), ("done", 0, 1), ("ysend", 3), ("fwd", 1, 0), ("wnear", 0),
    ("term", 0), ("own", 2, 2), ("tsend", 0), ("fwd", 2, 1), ("done", 1, 3), ("done", 1, 1),
    ("done", 1, 0), ("woth", 2), ("done", 1, 2), ("wfar",), ("fwd", 2, 3), ("term", 1),
    ("fwd", 2, 2), ("fwd", 2, 0), ("own", 3, 0), ("own", 3, 2), ("woth", 0), ("woth", 1),
    ("gadd", 0), ("own", 3, 3), ("tsend", 1), ("done", 2, 1), ("done", 2, 0), ("done", 2, 3),
    ("done", 2, 2), ("term", 2), ("gadd", 1), ("tsend", 2), ("fwd", 3, 0), ("fwd", 3, 2),
    ("own", 3, 1), ("done", 3, 2), ("fwd", 3, 3), ("gadd", 2), ("woth", 3), ("fwd", 3, 1),
    ("gsend", 2), ("done", 3, 0), ("done", 3, 3), ("gsend", 3), ("done", 3, 1), ("ladd", 3),
    ("gsend", 1), ("ladd", 2), ("ladd", 1), ("gsend", 0), ("lterms",), ("lsends",), ("gres",),
    ("pres",),
)


def back(j):
    return (4 - j) % 4


def kernel(
    gate_ref, up_ref, cot_ref, w_ref, gg_ref, ug_ref, gp_ref,
    gate_v, up_v, act_v, fac_v, hidh, hidt, cot_v, w_v, px_s, px_r, pown, pacc, ps, pq, pz, py,
    hg_acc, hg_s, hg_r, gg_v, ug_v, gp_v,
    ld, zl_s, zl_r, y_s, y_r, xr_s, xl_s, fl_r, fr_r, xf_s, xf_r, w_s, w_r, wc_s, wc_r,
    h_s, h_r, g_s, g_r, pc_s, pc_r, q_s, q_r, p_s, p_r, py_s, py_r, l_s, l_r, out_s, ready,
):
    dp, tn = lax.axis_index("dp"), lax.axis_index("tensor")
    c, y, zh = dp % 2, (dp // 2) % 4, dp // 8
    x, zl = tn // 2, tn % 2

    def plane(o, j):
        return ((((zh + o) % 4) * 4 + (y + j) % 4) * 2 + c, tn)

    other_core = (dp + 1 - 2 * c, tn)
    other_zl = (dp, tn + 1 - 2 * zl)
    right = (dp, ((x + 1) % 4) * 2 + zl)
    left = (dp, ((x + 3) % 4) * 2 + zl)

    def remote(src, dst, send, recv, device):
        return pltpu.make_async_remote_copy(
            src_ref=src, dst_ref=dst, send_sem=send, recv_sem=recv,
            device_id=device, device_id_type=MESH,
        )

    sent = []
    done_once = set()

    def start(copy):
        copy.start()
        sent.append(copy)

    def arrived(ref, recv, send):
        remote(ref, ref, send, recv, other_core).wait_recv()

    def chunk_cols(k):
        return pl.ds(pl.multiple_of(((zh + ORD[k]) % 4) * CHUNK, CHUNK), CHUNK)

    def rows_at(j, xx, n=64, extra=0):
        return pl.ds(pl.multiple_of(j * TOK + xx * 64 + extra, 32), n)

    near = [plane(0, j)[0] for j in (1, 2, 3)]
    near = [(d - c, tn) for d in near] + [(dp - c, d[1]) for d in (other_zl, right, left)]
    far = [(plane(o, 0)[0] - c + 1, tn) for o in (1, 3)]
    barrier = pltpu.get_barrier_semaphore()
    for peer in near + far:
        pl.semaphore_signal(barrier, inc=1, device_id=peer, device_id_type=MESH)

    @pl.when(c == 1)
    def _():
        pl.semaphore_signal(barrier, inc=1, device_id=other_core, device_id_type=MESH)

    def near_ready():
        @pl.when(c == 0)
        def _():
            pl.semaphore_wait(barrier, 2 * len(near) + 1)
            pl.semaphore_signal(ready, inc=1, device_id=other_core, device_id_type=MESH)

        @pl.when(c == 1)
        def _():
            pl.semaphore_wait(ready, 1)

    def far_ready():
        @pl.when(c == 1)
        def _():
            pl.semaphore_wait(barrier, 2 * len(far))
            pl.semaphore_signal(ready, inc=1, device_id=other_core, device_id_type=MESH)

        @pl.when(c == 0)
        def _():
            pl.semaphore_wait(ready, 1)

    own_rows = rows_at(0, x, 32, zl * 32)
    loads = []
    for k in range(4):
        loads.append(pltpu.make_async_copy(
            cot_ref.at[:, chunk_cols(k)], cot_v.at[k, own_rows], ld.at[k]))
    loads.append(pltpu.make_async_copy(gate_ref, gate_v, ld.at[4]))
    loads.append(pltpu.make_async_copy(up_ref, up_v, ld.at[5]))

    def quarter_rows(j):
        return pl.ds(pl.multiple_of(((y + j) % 4) * QUARTER, QUARTER), QUARTER)

    def w_rows(j):
        return pl.ds(pl.multiple_of(((y + j) % 2) * 64, 64), QUARTER)

    def w_cols(j, cc):
        return pl.ds(pl.multiple_of((((y + j) % 4) * 2 + cc) * SHARD, SHARD), SHARD)

    loads.append(pltpu.make_async_copy(
        w_ref.at[quarter_rows(0)], w_v.at[3, w_rows(0), w_cols(0, c)], ld.at[6]))
    for load in loads:
        load.start()
    pad = pl.ds(pl.multiple_of((1 - y % 2) * QUARTER, 64), 64)
    for k in range(4):
        w_v[k, pad, :] = jnp.zeros((64, CHUNK), BF16)
    near_ready()

    for k in range(4):
        start(remote(cot_ref.at[:, chunk_cols(k)], cot_v.at[k, own_rows],
                     zl_s.at[k], zl_r.at[k], other_zl))
    partner_rows = rows_at(0, x, 32, (1 - zl) * 32)

    def y_sends(k):
        loads[k].wait()
        arrived(cot_v.at[k, partner_rows], zl_r.at[k], zl_s.at[k])
        for j in ((2, 3, 1) if k == 3 else (1, 3, 2)):
            start(remote(cot_v.at[k, rows_at(0, x)], cot_v.at[k, rows_at(back(j), x)],
                         y_s.at[k, j], y_r.at[k, back(j)], plane(0, j)))

    def w_sends():
        for j in (1, 3, 2):
            start(remote(w_ref.at[quarter_rows(j)], w_v.at[3, w_rows(j), w_cols(0, c)],
                         w_s.at[3, back(j)], w_r.at[3, back(j)], plane(0, j)))

    def w_block(k, j, cc):
        return w_v.at[k, w_rows(0), w_cols(j, cc)]

    def w_arrived(k, j):
        if (k, j) == (3, 0):
            loads[6].wait()
        else:
            arrived(w_block(k, j, c), w_r.at[k, j], w_s.at[k, j])
        start(remote(w_block(k, j, c), w_block(k, j, c), wc_s.at[k, j], wc_r.at[k, j], other_core))

    def w_own(j):
        w_arrived(3, j)
        for o in (1, 3):
            k = SLOT[back(o)]
            start(remote(w_block(3, j, c), w_block(k, j, c), w_s.at[k, j], w_r.at[k, j],
                         plane(o, 0)))

    def w_near(j):
        for o, passed in ((3, (0, 1)), (1, (2, 3))):
            k = SLOT[back(o)]
            w_arrived(k, j)
            if j in passed:
                start(remote(w_block(k, j, c), w_block(SLOT[2], j, c),
                             w_s.at[SLOT[2], j], w_r.at[SLOT[2], j], plane(o, 0)))

    def w_far():
        for j in range(4):
            w_arrived(SLOT[2], j)

    def w_other(k):
        for j in range(4):
            arrived(w_block(k, j, 1 - c), wc_r.at[k, j], wc_s.at[k, j])

    HOME = (0, 4, 8, 11, 14)

    def home(part):
        if part == 0:
            loads[4].wait()
            loads[5].wait()

        def block(f, _):
            cols = pl.ds(pl.multiple_of(f * 128, 128), 128)
            g = gate_v[:, cols].astype(F32)
            u = up_v[:, cols].astype(F32)
            s = jax.nn.sigmoid(g)
            act = g * s
            act_v[:, cols] = act
            fac_v[:, cols] = u * s * (1.0 + g * (1.0 - s))
            hidh[cols, :] = (act * u).T.astype(BF16)
            return 0

        lax.fori_loop(HOME[part], HOME[part + 1], block, 0)

    def hidden_sends():
        for j in (2, 1, 3):
            start(remote(hidh.at[quarter_rows(j)], hidt.at[:, pl.ds(back(j) * TOK, TOK)],
                         h_s.at[j], h_r.at[back(j)], plane(0, j)))
        hidt[:, 0:TOK] = hidh[quarter_rows(0), :]

    def hidden_arrived():
        for j in (1, 3, 2):
            arrived(hidt.at[:, pl.ds(j * TOK, TOK)], h_r.at[j], h_s.at[j])

    def term(k):
        def tile(j, _):
            cols = pl.ds(pl.multiple_of(((y + j) % 4) * 256, 256), 256)
            part = jnp.dot(hidt[...], cot_v[k, :, cols], preferred_element_type=F32)
            low, high = part[:, :SHARD], part[:, SHARD:]
            pown[j] = jnp.where(c == 0, low, high)
            px_s[k, j] = jnp.where(c == 0, high, low).astype(BF16)
            return 0

        lax.fori_loop(0, 4, tile, 0)
        start(remote(px_s.at[k], px_r.at[k], pc_s.at[k], pc_r.at[k], other_core))

    def term_sends(k):
        arrived(px_r.at[k], pc_r.at[k], pc_s.at[k])
        if k:
            passed = (0, 1) if k == 1 else (2, 3)
            part = pl.ds(passed[0], 2)
            arrived(pq.at[part], q_r.at[k - 1], q_s.at[k - 1])
        for j in range(4):
            total = pown[j] + px_r[k, j].astype(F32)
            if k and j in passed:
                total = total + pq[j].astype(F32)
            ps[k, j] = total.astype(BF16)
        if k == 0:
            for n, o in enumerate((1, 3)):
                part = pl.ds(2 * n, 2)
                start(remote(ps.at[0, part], pq.at[part], q_s.at[n], q_r.at[n], plane(o, 0)))
        else:
            start(remote(ps.at[k], pz.at[k - 1], p_s.at[k], p_r.at[k], plane(ORD[k], 0)))

    def last_part(block, j):
        cols = pl.ds(pl.multiple_of(((y + j) % 4) * 256, 256), 256)
        return jnp.dot(hidt[:, pl.ds(block * TOK, TOK)], cot_v[3, pl.ds(block * TOK, TOK), cols],
                       preferred_element_type=F32)

    def last_add(block):
        first = ("ladd",) not in done_once
        done_once.add(("ladd",))

        def tile(j, _):
            part = last_part(block, j)
            pacc[j] = part if first else pacc[j] + part
            return 0

        lax.fori_loop(0, 4, tile, 0)

    def last_terms():
        for j in (2, 1, 3, 0):
            part = pacc[j] + last_part(0, j)
            low, high = part[:, :SHARD], part[:, SHARD:]
            px_s[3, j] = jnp.where(c == 0, high, low).astype(BF16)
            start(remote(px_s.at[3, j], px_r.at[3, j], l_s.at[j], l_r.at[j], other_core))
            pown[j] = jnp.where(c == 0, low, high)

    def last_sends():
        for k in (1, 2):
            arrived(pz.at[k - 1], p_r.at[k], p_s.at[k])
        for j in (2, 1, 3, 0):
            arrived(px_r.at[3, j], l_r.at[j], l_s.at[j])
            total = pown[j] + px_r[3, j].astype(F32) + (pz[0, j].astype(F32) + pz[1, j].astype(F32))
            if j:
                ps[3, j] = total.astype(BF16)
                start(remote(ps.at[3, j], py.at[back(j)], py_s.at[j], py_r.at[back(j)], plane(0, j)))
            else:
                gp_v[quarter_rows(0), :] = total * unscale

    def grad_part(k, j):
        rows = pl.ds(j * TOK, TOK) if isinstance(j, int) else pl.ds(pl.multiple_of(j * TOK, TOK), TOK)
        return lax.dot_general(cot_v[k, rows, :], w_v[k], (((1,), (1,)), ((), ())),
                               preferred_element_type=F32)

    def grad_add(k):
        first = ("gadd",) not in done_once
        done_once.add(("gadd",))

        def tile(j, _):
            part = grad_part(k, j)
            hg_acc[j] = part if first else hg_acc[j] + part
            return 0

        lax.fori_loop(0, 4, tile, 0)

    def grad_sends(j):
        hg_s[j] = (hg_acc[j] + grad_part(3, j)).astype(BF16)
        if j == 0:
            copy = pltpu.make_async_copy(hg_s.at[0], hg_r.at[y], g_r.at[y])
            copy.start()
        else:
            start(remote(hg_s.at[j], hg_r.at[y], g_s.at[j], g_r.at[y], plane(0, j)))

    def own(k, j):
        if j:
            arrived(cot_v.at[k, rows_at(j, x)], y_r.at[k, j], y_s.at[k, j])
        mine = cot_v.at[k, rows_at(j, x)]
        start(remote(mine, mine, xr_s.at[k, j], fl_r.at[k, j], right))
        start(remote(mine, mine, xl_s.at[k, j], fr_r.at[k, j], left))

    def forward(k, j):
        from_left = cot_v.at[k, rows_at(j, (x + 3) % 4)]
        from_right = cot_v.at[k, rows_at(j, (x + 1) % 4)]
        arrived(from_left, fl_r.at[k, j], xr_s.at[k, j])
        arrived(from_right, fr_r.at[k, j], xl_s.at[k, j])
        block, device = (from_left, right) if j in RIGHT else (from_right, left)
        start(remote(block, block, xf_s.at[k, j], xf_r.at[k, j], device))

    def done(k, j):
        arrived(cot_v.at[k, rows_at(j, (x + 2) % 4)], xf_r.at[k, j], xf_s.at[k, j])

    stores = []

    def result(r, _):
        rows = pl.ds(pl.multiple_of(r * 32, 32), 32)
        p = [hg_r[q, rows, :].astype(F32) for q in range(4)]
        grad = jnp.concatenate(
            [p[0][:, :384], p[0][:, 384:] + p[1][:, :128], p[1][:, 128:],
             p[2][:, :384], p[2][:, 384:] + p[3][:, :128], p[3][:, 128:]], axis=1)
        ug_v[rows, :] = (grad * act_v[rows, :]).astype(BF16)
        gg_v[rows, :] = (grad * fac_v[rows, :]).astype(BF16)
        return 0

    def grad_results():
        for yy in range(4):
            arrived(hg_r.at[yy], g_r.at[yy], g_s.at[0])
        for half in range(2):
            lax.fori_loop(half * 4, half * 4 + 4, result, 0)
            rows = pl.ds(half * 128, 128)
            for n, (src, dst) in enumerate(((ug_v, ug_ref), (gg_v, gg_ref))):
                stores.append(pltpu.make_async_copy(
                    src.at[rows], dst.at[rows], out_s.at[half * 2 + n]))
                stores[-1].start()

    def term_results():
        for j in (0, 1, 3, 2):
            if j:
                arrived(py.at[j], py_r.at[j], py_s.at[j])
                gp_v[quarter_rows(j), :] = py[j].astype(F32) * unscale
            stores.append(pltpu.make_async_copy(
                gp_v.at[quarter_rows(j)], gp_ref.at[quarter_rows(j)], out_s.at[4 + j]))
            stores[-1].start()

    steps = dict(
        ysend=y_sends, own=own, fwd=forward, done=done, wsend=w_sends, farr=far_ready, wown=w_own,
        wnear=w_near, wfar=w_far, woth=w_other, home=home, hsend=hidden_sends,
        harr=hidden_arrived, term=term, tsend=term_sends, gadd=grad_add, ladd=last_add,
        gsend=grad_sends, lterms=last_terms, lsends=last_sends, gres=grad_results,
        pres=term_results,
    )
    for name, *place in ORDER:
        steps[name](*place)
    for copy in sent:
        copy.wait_send()
    for store in stores:
        store.wait()


def grads(gate_pre, up_pre, cotangent, w_prev):
    def dma(*shape):
        return pltpu.SemaphoreType.DMA(shape)

    any_spec = pl.BlockSpec(memory_space=pl.ANY)
    scratch = [
        pltpu.VMEM((TOK, HID), BF16),
        pltpu.VMEM((TOK, HID), BF16),
        pltpu.VMEM((TOK, HID), F32),
        pltpu.VMEM((TOK, HID), F32),
        pltpu.VMEM((HID, TOK), BF16),
        pltpu.VMEM((QUARTER, 4 * TOK), BF16),
        pltpu.VMEM((4, 4 * TOK, CHUNK), BF16),
        pltpu.VMEM((4, WIDE, CHUNK), BF16),
        pltpu.VMEM((4, 4, QUARTER, SHARD), BF16),
        pltpu.VMEM((4, 4, QUARTER, SHARD), BF16),
        pltpu.VMEM((4, QUARTER, SHARD), F32),
        pltpu.VMEM((4, QUARTER, 256), F32),
        pltpu.VMEM((4, 4, QUARTER, SHARD), BF16),
        pltpu.VMEM((4, QUARTER, SHARD), BF16),
        pltpu.VMEM((2, 4, QUARTER, SHARD), BF16),
        pltpu.VMEM((4, QUARTER, SHARD), BF16),
        pltpu.VMEM((4, TOK, WIDE), F32),
        pltpu.VMEM((4, TOK, WIDE), BF16),
        pltpu.VMEM((4, TOK, WIDE), BF16),
        pltpu.VMEM((TOK, HID), BF16),
        pltpu.VMEM((TOK, HID), BF16),
        pltpu.VMEM((HID, SHARD), F32),
        dma(8), dma(4), dma(4), dma(4, 4), dma(4, 4),
        dma(4, 4), dma(4, 4), dma(4, 4), dma(4, 4), dma(4, 4), dma(4, 4),
        dma(4, 4), dma(4, 4), dma(4, 4), dma(4, 4),
        dma(4), dma(4), dma(4), dma(4),
        dma(4), dma(4), dma(2), dma(2), dma(4), dma(4), dma(4), dma(4),
        dma(4), dma(4), dma(8),
        pltpu.SemaphoreType.REGULAR,
    ]
    return pl.pallas_call(
        kernel,
        out_shape=(
            jax.ShapeDtypeStruct((TOK, HID), BF16),
            jax.ShapeDtypeStruct((TOK, HID), BF16),
            jax.ShapeDtypeStruct((HID, SHARD), F32),
        ),
        in_specs=[any_spec] * 4,
        out_specs=(any_spec,) * 3,
        scratch_shapes=scratch,
        compiler_params=pltpu.CompilerParams(
            collective_id=0, has_side_effects=True, vmem_limit_bytes=62 * 2**20
        ),
        cost_estimate=pl.CostEstimate(
            flops=4 * TOK * HID * 4096, bytes_accessed=8 * 2**20, transcendentals=TOK * HID
        ),
    )(gate_pre, up_pre, cotangent, w_prev)


def body(gate_pre, up_pre, cotangent, w_prev, param_next, grad_next, moment_one, moment_two):
    gate_grad, up_grad, grad_prev = grads(gate_pre, up_pre, cotangent, w_prev)
    moment_one_f = beta_first * moment_one.astype(jnp.float32) + (1.0 - beta_first) * grad_next
    moment_two_f = (
        beta_second * moment_two.astype(jnp.float32) + (1.0 - beta_second) * grad_next * grad_next
    )
    first_fix = 1.0 - beta_first**STEP
    second_fix = 1.0 - beta_second**STEP
    adam_step = (
        moment_one_f / first_fix / (jnp.sqrt(moment_two_f / second_fix) + epsilon)
        + decay_rate * param_next
    )
    param_new = param_next - learn_rate * adam_step
    return (
        gate_grad,
        up_grad,
        grad_prev,
        param_new,
        moment_one_f.astype(jnp.bfloat16),
        moment_two_f.astype(jnp.bfloat16),
        adam_step,
    )


def solution(mesh):
    in_specs = (
        P("dp", "tensor"),
        P("dp", "tensor"),
        P(("dp", "tensor"), None),
        P("tensor", "dp"),
        P("tensor", "dp"),
        P("tensor", "dp"),
        P("tensor", "dp"),
        P("tensor", "dp"),
    )
    out_specs = (
        P("dp", "tensor"),
        P("dp", "tensor"),
        P("tensor", "dp"),
        P("tensor", "dp"),
        P("tensor", "dp"),
        P("tensor", "dp"),
        P("tensor", "dp"),
    )
    return jax.shard_map(body, mesh=mesh, in_specs=in_specs, out_specs=out_specs, check_vma=False)
```

```python
import jax
import jax.numpy as jnp
from jax import lax
from jax.experimental import pallas as pl
from jax.experimental.pallas import tpu as pltpu
from jax.sharding import PartitionSpec as P

STEP = 10


beta_first = 0.9
beta_second = 0.95
epsilon = 1e-08
decay_rate = 0.1
learn_rate = 0.0003
unscale = 1.0 / 32.0

MESH = pl.DeviceIdType.MESH
F32, BF16 = jnp.float32, jnp.bfloat16

TOK, HID, QUARTER, WIDE, CHUNK, SHARD = 256, 1792, 448, 512, 1024, 128
ORD = (2, 1, 3, 0)
SLOT = {o: k for k, o in enumerate(ORD)}
RIGHT = (0, 3)
ALONG_X = 2
ORDER = (
    ("wsend",), ("ysend", 0), ("own", 0, 0), ("home", 0), ("home", 1), ("home", 2), ("home", 3),
    ("hsend",), ("farr",), ("bown",), ("wown", 0), ("wown", 2), ("own", 0, 3), ("wown", 3),
    ("ysend", 1), ("own", 0, 1), ("own", 0, 2), ("fwd", 0, 0), ("fwd", 0, 3), ("wown", 1),
    ("fwd", 0, 1), ("fwd", 0, 2), ("bfwd",), ("ysend", 3), ("own", 1, 3), ("wnear", 0),
    ("own", 1, 0), ("done", 0, 2), ("done", 0, 3), ("by", 1), ("done", 0, 0), ("wnear", 2),
    ("harr",), ("own", 1, 1), ("done", 0, 1), ("term", 0), ("tsend", 0), ("by", 2), ("own", 1, 2),
    ("fwd", 1, 3), ("wnear", 1), ("fwd", 1, 0), ("fwd", 1, 1), ("fwd", 1, 2), ("done", 1, 3),
    ("by", 0), ("woth", 3), ("own", 3, 3), ("wnear", 3), ("woth", 2), ("done", 1, 2), ("woth", 1),
    ("own", 3, 2), ("done", 1, 0), ("done", 1, 1), ("term", 1), ("own", 3, 0), ("own", 3, 1),
    ("by", 3), ("tsend", 1), ("fwd", 3, 2), ("gadd", 1), ("fwd", 3, 3), ("wfar",), ("bdone",),
    ("term", 2), ("done", 3, 3), ("ladd", 3), ("fwd", 3, 0), ("fwd", 3, 1), ("woth", 0),
    ("gadd", 2), ("done", 3, 2), ("tsend", 2), ("gadd", 0), ("gsend", 2), ("gsend", 3),
    ("ladd", 2), ("done", 3, 0), ("done", 3, 1), ("ladd", 1), ("gsend", 1), ("lterms",),
    ("lsends",), ("gsend", 0), ("gres",), ("pres",),
)


def back(j):
    return (4 - j) % 4


def kernel(
    gate_ref, up_ref, cot_ref, w_ref, gg_ref, ug_ref, gp_ref,
    gate_v, up_v, act_v, fac_v, hidh, hidt, cot_v, w_v, px_s, px_r, pown, pacc, ps, pq, pz, py,
    hg_acc, hg_s, hg_r, gg_v, ug_v, gp_v,
    ld, zl_s, zl_r, y_s, y_r, xr_s, xl_s, fl_r, fr_r, xf_s, xf_r, w_s, w_r, wc_s, wc_r,
    h_s, h_r, g_s, g_r, pc_s, pc_r, q_s, q_r, p_s, p_r, py_s, py_r, l_s, l_r, by_s, by_r, out_s, ready,
):
    dp, tn = lax.axis_index("dp"), lax.axis_index("tensor")
    c, y, zh = dp % 2, (dp // 2) % 4, dp // 8
    x, zl = tn // 2, tn % 2

    def plane(o, j):
        return ((((zh + o) % 4) * 4 + (y + j) % 4) * 2 + c, tn)

    other_core = (dp + 1 - 2 * c, tn)
    other_zl = (dp, tn + 1 - 2 * zl)
    right = (dp, ((x + 1) % 4) * 2 + zl)
    left = (dp, ((x + 3) % 4) * 2 + zl)

    def remote(src, dst, send, recv, device):
        return pltpu.make_async_remote_copy(
            src_ref=src, dst_ref=dst, send_sem=send, recv_sem=recv,
            device_id=device, device_id_type=MESH,
        )

    sent = []
    done_once = set()

    def start(copy):
        copy.start()
        sent.append(copy)

    def arrived(ref, recv, send):
        remote(ref, ref, send, recv, other_core).wait_recv()

    def features(o, first, n):
        return pl.ds(pl.multiple_of(((zh + o) % 4) * CHUNK + first, 512), n)

    def rows_at(j, xx, n=64, extra=0):
        return pl.ds(pl.multiple_of(j * TOK + xx * 64 + extra, 32), n)

    near = [plane(0, j)[0] for j in (1, 2, 3)]
    near = [(d - c, tn) for d in near] + [(dp - c, d[1]) for d in (other_zl, right, left)]
    far = [(plane(o, 0)[0] - c + 1, tn) for o in (1, 3)]
    barrier = pltpu.get_barrier_semaphore()
    for peer in near + far:
        pl.semaphore_signal(barrier, inc=1, device_id=peer, device_id_type=MESH)

    @pl.when(c == 1)
    def _():
        pl.semaphore_signal(barrier, inc=1, device_id=other_core, device_id_type=MESH)

    def near_ready():
        @pl.when(c == 0)
        def _():
            pl.semaphore_wait(barrier, 2 * len(near) + 1)
            pl.semaphore_signal(ready, inc=1, device_id=other_core, device_id_type=MESH)

        @pl.when(c == 1)
        def _():
            pl.semaphore_wait(ready, 1)

    def far_ready():
        @pl.when(c == 1)
        def _():
            pl.semaphore_wait(barrier, 2 * len(far))
            pl.semaphore_signal(ready, inc=1, device_id=other_core, device_id_type=MESH)

        @pl.when(c == 0)
        def _():
            pl.semaphore_wait(ready, 1)

    own_rows = rows_at(0, x, 32, zl * 32)
    loads = []
    for k in range(4):
        if k in (1, 2):
            parts = [(o, (k - 1) * 512, 512, to) for o, to in ((1, 0), (3, 512))]
        else:
            parts = [(ORD[k], 0, CHUNK, 0)]
        for o, first, n, to in parts:
            sem = ld.at[k] if to == 0 else ld.at[6 + k]
            loads.append(pltpu.make_async_copy(
                cot_ref.at[:, features(o, first, n)], cot_v.at[k, own_rows, pl.ds(to, n)], sem))
    cot_loads = ((0,), (1, 2), (3, 4), (5,))
    gate_load, up_load, w_load = 6, 7, 8
    loads.append(pltpu.make_async_copy(gate_ref, gate_v, ld.at[4]))
    loads.append(pltpu.make_async_copy(up_ref, up_v, ld.at[5]))

    def quarter_rows(j):
        return pl.ds(pl.multiple_of(((y + j) % 4) * QUARTER, QUARTER), QUARTER)

    def w_rows(j):
        return pl.ds(pl.multiple_of(((y + j) % 2) * 64, 64), QUARTER)

    def w_cols(j, cc):
        return pl.ds(pl.multiple_of((((y + j) % 4) * 2 + cc) * SHARD, SHARD), SHARD)

    loads.append(pltpu.make_async_copy(
        w_ref.at[quarter_rows(0)], w_v.at[3, w_rows(0), w_cols(0, c)], ld.at[6]))
    for load in loads:
        load.start()
    pad = pl.ds(pl.multiple_of((1 - y % 2) * QUARTER, 64), 64)
    for k in range(4):
        w_v[k, pad, :] = jnp.zeros((64, CHUNK), BF16)
    near_ready()

    for k in range(4):
        for n in cot_loads[k]:
            loads[n].wait()
        mine = cot_v.at[k, own_rows]
        start(remote(mine, mine, zl_s.at[k], zl_r.at[k], other_zl))
    partner_rows = rows_at(0, x, 32, (1 - zl) * 32)

    def y_sends(k):
        arrived(cot_v.at[k, partner_rows], zl_r.at[k], zl_s.at[k])
        for j in ((2, 3, 1) if k == 3 else (1, 3, 2)):
            start(remote(cot_v.at[k, rows_at(0, x)], cot_v.at[k, rows_at(back(j), x)],
                         y_s.at[k, j], y_r.at[k, back(j)], plane(0, j)))

    def w_sends():
        for j in (1, 3, 2):
            start(remote(w_ref.at[quarter_rows(j)], w_v.at[3, w_rows(j), w_cols(0, c)],
                         w_s.at[3, back(j)], w_r.at[3, back(j)], plane(0, j)))

    def w_block(k, j, cc):
        if k in (1, 2):
            yy = (y + j) % 4
            col = (k - 1) * 512 + (yy % 2) * 256 + cc * SHARD
            return w_v.at[1 + yy // 2, w_rows(0), pl.ds(pl.multiple_of(col, SHARD), SHARD)]
        return w_v.at[k, w_rows(0), w_cols(j, cc)]

    def w_arrived(k, j):
        if (k, j) == (3, 0):
            loads[w_load].wait()
        else:
            arrived(w_block(k, j, c), w_r.at[k, j], w_s.at[k, j])
        start(remote(w_block(k, j, c), w_block(k, j, c), wc_s.at[k, j], wc_r.at[k, j], other_core))

    def w_own(j):
        w_arrived(3, j)
        for o in (1, 3):
            k = SLOT[back(o)]
            start(remote(w_block(3, j, c), w_block(k, j, c), w_s.at[k, j], w_r.at[k, j],
                         plane(o, 0)))

    def w_near(j):
        for o, passed in ((3, (0, 1)), (1, (2, 3))):
            k = SLOT[back(o)]
            w_arrived(k, j)
            if j in passed:
                start(remote(w_block(k, j, c), w_block(SLOT[2], j, c),
                             w_s.at[SLOT[2], j], w_r.at[SLOT[2], j], plane(o, 0)))

    def w_far():
        for j in range(4):
            w_arrived(SLOT[2], j)

    def w_other(k):
        for j in range(4):
            arrived(w_block(k, j, 1 - c), wc_r.at[k, j], wc_s.at[k, j])

    HOME = (0, 4, 8, 11, 14)

    def home(part):
        if part == 0:
            loads[gate_load].wait()
            loads[up_load].wait()

        def block(f, _):
            cols = pl.ds(pl.multiple_of(f * 128, 128), 128)
            g = gate_v[:, cols].astype(F32)
            u = up_v[:, cols].astype(F32)
            s = jax.nn.sigmoid(g)
            act = g * s
            act_v[:, cols] = act
            fac_v[:, cols] = u * s * (1.0 + g * (1.0 - s))
            hidh[cols, :] = (act * u).T.astype(BF16)
            return 0

        lax.fori_loop(HOME[part], HOME[part + 1], block, 0)

    def hidden_sends():
        for j in (2, 1, 3):
            start(remote(hidh.at[quarter_rows(j)], hidt.at[:, pl.ds(back(j) * TOK, TOK)],
                         h_s.at[j], h_r.at[back(j)], plane(0, j)))
        hidt[:, 0:TOK] = hidh[quarter_rows(0), :]

    def hidden_arrived():
        for j in (1, 3, 2):
            arrived(hidt.at[:, pl.ds(j * TOK, TOK)], h_r.at[j], h_s.at[j])

    def term(k):
        def tile(j, _):
            cols = pl.ds(pl.multiple_of(j * 256, 256), 256)
            part = jnp.dot(hidt[...], cot_v[k, :, cols], preferred_element_type=F32)
            low, high = part[:, :SHARD], part[:, SHARD:]
            pown[j] = jnp.where(c == 0, low, high)
            px_s[k, j] = jnp.where(c == 0, high, low).astype(BF16)
            return 0

        lax.fori_loop(0, 4, tile, 0)
        start(remote(px_s.at[k], px_r.at[k], pc_s.at[k], pc_r.at[k], other_core))

    def term_sends(k):
        arrived(px_r.at[k], pc_r.at[k], pc_s.at[k])
        if k:
            part = pl.ds(2 * (k - 1), 2)
            arrived(pq.at[part], q_r.at[k - 1], q_s.at[k - 1])
        for t in range(4):
            total = pown[t] + px_r[k, t].astype(F32)
            if k and t // 2 == k - 1:
                total = total + pq[t].astype(F32)
            ps[k, t] = total.astype(BF16)
        for n, o in enumerate((1, 3)):
            part = pl.ds(2 * n, 2)
            if k == 0:
                start(remote(ps.at[0, part], pq.at[part], q_s.at[n], q_r.at[n], plane(o, 0)))
            else:
                start(remote(ps.at[k, part], pz.at[n, pl.ds(2 * (k - 1), 2)],
                             p_s.at[k, n], p_r.at[k, n], plane(o, 0)))

    def last_part(block, j):
        cols = pl.ds(pl.multiple_of(((y + j) % 4) * 256, 256), 256)
        return jnp.dot(hidt[:, pl.ds(block * TOK, TOK)], cot_v[3, pl.ds(block * TOK, TOK), cols],
                       preferred_element_type=F32)

    def last_add(block):
        first = ("ladd",) not in done_once
        done_once.add(("ladd",))

        def tile(j, _):
            part = last_part(block, j)
            pacc[j] = part if first else pacc[j] + part
            return 0

        lax.fori_loop(0, 4, tile, 0)

    def last_terms():
        for j in (2, 1, 3, 0):
            part = pacc[j] + last_part(0, j)
            low, high = part[:, :SHARD], part[:, SHARD:]
            px_s[3, j] = jnp.where(c == 0, high, low).astype(BF16)
            start(remote(px_s.at[3, j], px_r.at[3, j], l_s.at[j], l_r.at[j], other_core))
            pown[j] = jnp.where(c == 0, low, high)

    def last_sends():
        for k in (1, 2):
            for n in range(2):
                arrived(pz.at[n, pl.ds(2 * (k - 1), 2)], p_r.at[k, n], p_s.at[k, n])
        for j in (2, 1, 3, 0):
            arrived(px_r.at[3, j], l_r.at[j], l_s.at[j])
            yy = (y + j) % 4
            total = pown[j] + px_r[3, j].astype(F32) + (pz[0, yy].astype(F32) + pz[1, yy].astype(F32))
            if j:
                ps[3, j] = total.astype(BF16)
                start(remote(ps.at[3, j], py.at[back(j)], py_s.at[j], py_r.at[back(j)], plane(0, j)))
            else:
                gp_v[quarter_rows(0), :] = total * unscale

    def grad_part(k, j):
        rows = pl.ds(j * TOK, TOK) if isinstance(j, int) else pl.ds(pl.multiple_of(j * TOK, TOK), TOK)
        return lax.dot_general(cot_v[k, rows, :], w_v[k], (((1,), (1,)), ((), ())),
                               preferred_element_type=F32)

    def grad_add(k):
        first = ("gadd",) not in done_once
        done_once.add(("gadd",))

        def tile(j, _):
            part = grad_part(k, j)
            hg_acc[j] = part if first else hg_acc[j] + part
            return 0

        lax.fori_loop(0, 4, tile, 0)

    def grad_sends(j):
        hg_s[j] = (hg_acc[j] + grad_part(3, j)).astype(BF16)
        if j == 0:
            copy = pltpu.make_async_copy(hg_s.at[0], hg_r.at[y], g_r.at[y])
            copy.start()
        else:
            start(remote(hg_s.at[j], hg_r.at[y], g_s.at[j], g_r.at[y], plane(0, j)))

    def own(k, j):
        if j:
            arrived(cot_v.at[k, rows_at(j, x)], y_r.at[k, j], y_s.at[k, j])
        mine = cot_v.at[k, rows_at(j, x)]
        start(remote(mine, mine, xr_s.at[k, j], fl_r.at[k, j], right))
        start(remote(mine, mine, xl_s.at[k, j], fr_r.at[k, j], left))

    def forward(k, j):
        from_left = cot_v.at[k, rows_at(j, (x + 3) % 4)]
        from_right = cot_v.at[k, rows_at(j, (x + 1) % 4)]
        arrived(from_left, fl_r.at[k, j], xr_s.at[k, j])
        arrived(from_right, fr_r.at[k, j], xl_s.at[k, j])
        block, device = (from_left, right) if j in RIGHT else (from_right, left)
        start(remote(block, block, xf_s.at[k, j], xf_r.at[k, j], device))

    def done(k, j):
        arrived(cot_v.at[k, rows_at(j, (x + 2) % 4)], xf_r.at[k, j], xf_s.at[k, j])

    stores = []

    def result(r, _):
        rows = pl.ds(pl.multiple_of(r * 32, 32), 32)
        p = [hg_r[q, rows, :].astype(F32) for q in range(4)]
        grad = jnp.concatenate(
            [p[0][:, :384], p[0][:, 384:] + p[1][:, :128], p[1][:, 128:],
             p[2][:, :384], p[2][:, 384:] + p[3][:, :128], p[3][:, 128:]], axis=1)
        ug_v[rows, :] = (grad * act_v[rows, :]).astype(BF16)
        gg_v[rows, :] = (grad * fac_v[rows, :]).astype(BF16)
        return 0

    def grad_results():
        for yy in range(4):
            arrived(hg_r.at[yy], g_r.at[yy], g_s.at[0])
        for half in range(2):
            lax.fori_loop(half * 4, half * 4 + 4, result, 0)
            rows = pl.ds(half * 128, 128)
            for n, (src, dst) in enumerate(((ug_v, ug_ref), (gg_v, gg_ref))):
                stores.append(pltpu.make_async_copy(
                    src.at[rows], dst.at[rows], out_s.at[half * 2 + n]))
                stores[-1].start()

    def term_results():
        for j in (0, 1, 3, 2):
            if j:
                arrived(py.at[j], py_r.at[j], py_s.at[j])
                gp_v[quarter_rows(j), :] = py[j].astype(F32) * unscale
            stores.append(pltpu.make_async_copy(
                gp_v.at[quarter_rows(j)], gp_ref.at[quarter_rows(j)], out_s.at[4 + j]))
            stores[-1].start()

    def b_rows(j, n, first=0, size=64):
        return rows_at(j, (x + (0, 3, 1, 2)[n]) % 4, size, first)

    def b_ref(*rows):
        return cot_v.at[ALONG_X, b_rows(*rows)]

    def b_own():
        arrived(cot_v.at[ALONG_X, partner_rows], zl_r.at[ALONG_X], zl_s.at[ALONG_X])
        mine = b_ref(0, 0)
        start(remote(mine, mine, xr_s.at[ALONG_X, 0], fl_r.at[ALONG_X, 0], right))
        start(remote(mine, mine, xl_s.at[ALONG_X, 0], fr_r.at[ALONG_X, 0], left))

    def b_forward():
        arrived(b_ref(0, 1), fl_r.at[ALONG_X, 0], xr_s.at[ALONG_X, 0])
        arrived(b_ref(0, 2), fr_r.at[ALONG_X, 0], xl_s.at[ALONG_X, 0])
        for n, device in ((1, right), (2, left)):
            half = b_ref(0, n, 32 * (n - 1), 32)
            start(remote(half, half, xf_s.at[ALONG_X, n], xf_r.at[ALONG_X, n], device))

    def b_y(n):
        if n == 3:
            for m in (1, 2):
                arrived(b_ref(0, 3, 32 * (m - 1), 32), xf_r.at[ALONG_X, m], xf_s.at[ALONG_X, m])
        for j in (1, 3, 2):
            start(remote(b_ref(0, n), b_ref(back(j), n), by_s.at[n, j], by_r.at[n, back(j)],
                         plane(0, j)))

    def b_done():
        for n in range(4):
            for j in (1, 3, 2):
                arrived(b_ref(j, n), by_r.at[n, j], by_s.at[n, j])

    steps = dict(
        bown=b_own, bfwd=b_forward, by=b_y, bdone=b_done,
        ysend=y_sends, own=own, fwd=forward, done=done, wsend=w_sends, farr=far_ready, wown=w_own,
        wnear=w_near, wfar=w_far, woth=w_other, home=home, hsend=hidden_sends,
        harr=hidden_arrived, term=term, tsend=term_sends, gadd=grad_add, ladd=last_add,
        gsend=grad_sends, lterms=last_terms, lsends=last_sends, gres=grad_results,
        pres=term_results,
    )
    for name, *place in ORDER:
        steps[name](*place)
    for copy in sent:
        copy.wait_send()
    for store in stores:
        store.wait()


def grads(gate_pre, up_pre, cotangent, w_prev):
    def dma(*shape):
        return pltpu.SemaphoreType.DMA(shape)

    any_spec = pl.BlockSpec(memory_space=pl.ANY)
    scratch = [
        pltpu.VMEM((TOK, HID), BF16),
        pltpu.VMEM((TOK, HID), BF16),
        pltpu.VMEM((TOK, HID), F32),
        pltpu.VMEM((TOK, HID), F32),
        pltpu.VMEM((HID, TOK), BF16),
        pltpu.VMEM((QUARTER, 4 * TOK), BF16),
        pltpu.VMEM((4, 4 * TOK, CHUNK), BF16),
        pltpu.VMEM((4, WIDE, CHUNK), BF16),
        pltpu.VMEM((4, 4, QUARTER, SHARD), BF16),
        pltpu.VMEM((4, 4, QUARTER, SHARD), BF16),
        pltpu.VMEM((4, QUARTER, SHARD), F32),
        pltpu.VMEM((4, QUARTER, 256), F32),
        pltpu.VMEM((4, 4, QUARTER, SHARD), BF16),
        pltpu.VMEM((4, QUARTER, SHARD), BF16),
        pltpu.VMEM((2, 4, QUARTER, SHARD), BF16),
        pltpu.VMEM((4, QUARTER, SHARD), BF16),
        pltpu.VMEM((4, TOK, WIDE), F32),
        pltpu.VMEM((4, TOK, WIDE), BF16),
        pltpu.VMEM((4, TOK, WIDE), BF16),
        pltpu.VMEM((TOK, HID), BF16),
        pltpu.VMEM((TOK, HID), BF16),
        pltpu.VMEM((HID, SHARD), F32),
        dma(10), dma(4), dma(4), dma(4, 4), dma(4, 4),
        dma(4, 4), dma(4, 4), dma(4, 4), dma(4, 4), dma(4, 4), dma(4, 4),
        dma(4, 4), dma(4, 4), dma(4, 4), dma(4, 4),
        dma(4), dma(4), dma(4), dma(4),
        dma(4), dma(4), dma(2), dma(2), dma(3, 2), dma(3, 2), dma(4), dma(4),
        dma(4), dma(4), dma(4, 4), dma(4, 4), dma(8),
        pltpu.SemaphoreType.REGULAR,
    ]
    return pl.pallas_call(
        kernel,
        out_shape=(
            jax.ShapeDtypeStruct((TOK, HID), BF16),
            jax.ShapeDtypeStruct((TOK, HID), BF16),
            jax.ShapeDtypeStruct((HID, SHARD), F32),
        ),
        in_specs=[any_spec] * 4,
        out_specs=(any_spec,) * 3,
        scratch_shapes=scratch,
        compiler_params=pltpu.CompilerParams(
            collective_id=0, has_side_effects=True, vmem_limit_bytes=62 * 2**20
        ),
        cost_estimate=pl.CostEstimate(
            flops=4 * TOK * HID * 4096, bytes_accessed=8 * 2**20, transcendentals=TOK * HID
        ),
    )(gate_pre, up_pre, cotangent, w_prev)


def finish_kernel(
    gg, ug, gp, param, grad, one, two, gg_out, ug_out, gp_out, param_out, one_out, two_out, step_out
):
    gg_out[...] = gg[...]
    ug_out[...] = ug[...]
    gp_out[...] = gp[...]
    g = grad[...]
    moment_one_f = beta_first * one[...].astype(F32) + (1.0 - beta_first) * g
    moment_two_f = beta_second * two[...].astype(F32) + (1.0 - beta_second) * g * g
    first_fix = 1.0 - beta_first**STEP
    second_fix = 1.0 - beta_second**STEP
    adam_step = (
        moment_one_f / first_fix / (jnp.sqrt(moment_two_f / second_fix) + epsilon)
        + decay_rate * param[...]
    )
    param_out[...] = param[...] - learn_rate * adam_step
    one_out[...] = moment_one_f.astype(BF16)
    two_out[...] = moment_two_f.astype(BF16)
    step_out[...] = adam_step


def finish(gate_grad, up_grad, grad_prev, param_next, grad_next, moment_one, moment_two):
    parts = 2
    tokens = pl.BlockSpec((TOK // parts, HID), lambda i: (i, 0))
    part = pl.BlockSpec((HID // parts, SHARD), lambda i: (i, 0))

    def like(*arrays):
        return tuple(jax.ShapeDtypeStruct(a.shape, a.dtype) for a in arrays)

    return pl.pallas_call(
        finish_kernel,
        grid=(parts,),
        out_shape=like(gate_grad, up_grad, grad_prev, param_next, moment_one, moment_two, param_next),
        in_specs=[tokens] * 2 + [part] * 5,
        out_specs=(tokens,) * 2 + (part,) * 5,
        cost_estimate=pl.CostEstimate(
            flops=20 * HID * SHARD, bytes_accessed=12 * 2**20, transcendentals=2 * HID * SHARD
        ),
    )(gate_grad, up_grad, grad_prev, param_next, grad_next, moment_one, moment_two)


def body(gate_pre, up_pre, cotangent, w_prev, param_next, grad_next, moment_one, moment_two):
    partial = grads(gate_pre, up_pre, cotangent, w_prev)
    return finish(*partial, param_next, grad_next, moment_one, moment_two)


def solution(mesh):
    in_specs = (
        P("dp", "tensor"),
        P("dp", "tensor"),
        P(("dp", "tensor"), None),
        P("tensor", "dp"),
        P("tensor", "dp"),
        P("tensor", "dp"),
        P("tensor", "dp"),
        P("tensor", "dp"),
    )
    out_specs = (
        P("dp", "tensor"),
        P("dp", "tensor"),
        P("tensor", "dp"),
        P("tensor", "dp"),
        P("tensor", "dp"),
        P("tensor", "dp"),
        P("tensor", "dp"),
    )
    return jax.shard_map(body, mesh=mesh, in_specs=in_specs, out_specs=out_specs, check_vma=False)
```

```python
import jax
import jax.numpy as jnp
from jax import lax
from jax.experimental import pallas as pl
from jax.experimental.pallas import tpu as pltpu
from jax.sharding import PartitionSpec as P

STEP = 10


beta_first = 0.9
beta_second = 0.95
epsilon = 1e-08
decay_rate = 0.1
learn_rate = 0.0003
unscale = 1.0 / 32.0

MESH = pl.DeviceIdType.MESH
F32, BF16 = jnp.float32, jnp.bfloat16

TOK, HID, QUARTER, WIDE, CHUNK, SHARD = 256, 1792, 448, 512, 1024, 128
ORD = (2, 1, 3, 0)
SLOT = {o: k for k, o in enumerate(ORD)}
RIGHT = (0, 3)
ALONG_X = 2
ORDER = (
    ("wsend",), ("ysend", 0), ("own", 0, 0), ("home", 0), ("home", 1), ("home", 2), ("home", 3),
    ("hsend",), ("farr",), ("bown",), ("wown", 0), ("wown", 2), ("own", 0, 3), ("wown", 3),
    ("ysend", 1), ("own", 0, 1), ("own", 0, 2), ("fwd", 0, 0), ("fwd", 0, 3), ("wown", 1),
    ("fwd", 0, 1), ("fwd", 0, 2), ("bfwd",), ("ysend", 3), ("own", 1, 3), ("wnear", 0),
    ("own", 1, 0), ("done", 0, 2), ("done", 0, 3), ("by", 1), ("done", 0, 0), ("wnear", 2),
    ("harr",), ("own", 1, 1), ("done", 0, 1), ("term", 0), ("tsend", 0), ("by", 2), ("own", 1, 2),
    ("fwd", 1, 3), ("wnear", 1), ("fwd", 1, 0), ("fwd", 1, 1), ("fwd", 1, 2), ("done", 1, 3),
    ("by", 0), ("woth", 3), ("own", 3, 3), ("wnear", 3), ("woth", 2), ("done", 1, 2), ("woth", 1),
    ("own", 3, 2), ("done", 1, 0), ("done", 1, 1), ("term", 1), ("own", 3, 0), ("own", 3, 1),
    ("by", 3), ("tsend", 1), ("fwd", 3, 2), ("gadd", 1), ("fwd", 3, 3), ("wfar",), ("bdone",),
    ("term", 2), ("done", 3, 3), ("ladd", 3), ("fwd", 3, 0), ("fwd", 3, 1), ("woth", 0),
    ("tsend", 2), ("gadd", 2), ("done", 3, 2), ("gadd", 0), ("gsend", 2), ("gsend", 3),
    ("ladd", 2), ("done", 3, 0), ("done", 3, 1), ("ladd", 1), ("gsend", 1), ("lterms",),
    ("lsends",), ("gsend", 0), ("gres",), ("pres",),
)


def back(j):
    return (4 - j) % 4


def kernel(
    gate_ref, up_ref, cot_ref, w_ref, gg_ref, ug_ref, gp_ref,
    gate_v, up_v, act_v, fac_v, hidh, hidt, cot_v, w_v, px_s, px_r, pown, pacc, ps, pq, pz, py,
    hg_acc, hg_s, hg_r, gg_v, ug_v, gp_v,
    ld, zl_s, zl_r, y_s, y_r, xr_s, xl_s, fl_r, fr_r, xf_s, xf_r, w_s, w_r, wc_s, wc_r,
    h_s, h_r, g_s, g_r, pc_s, pc_r, q_s, q_r, p_s, p_r, py_s, py_r, l_s, l_r, by_s, by_r, out_s, ready,
):
    dp, tn = lax.axis_index("dp"), lax.axis_index("tensor")
    c, y, zh = dp % 2, (dp // 2) % 4, dp // 8
    x, zl = tn // 2, tn % 2

    def plane(o, j):
        return ((((zh + o) % 4) * 4 + (y + j) % 4) * 2 + c, tn)

    other_core = (dp + 1 - 2 * c, tn)
    other_zl = (dp, tn + 1 - 2 * zl)
    right = (dp, ((x + 1) % 4) * 2 + zl)
    left = (dp, ((x + 3) % 4) * 2 + zl)

    def remote(src, dst, send, recv, device):
        return pltpu.make_async_remote_copy(
            src_ref=src, dst_ref=dst, send_sem=send, recv_sem=recv,
            device_id=device, device_id_type=MESH,
        )

    sent = []
    done_once = set()

    def start(copy):
        copy.start()
        sent.append(copy)

    def arrived(ref, recv, send):
        remote(ref, ref, send, recv, other_core).wait_recv()

    def features(o, first, n):
        return pl.ds(pl.multiple_of(((zh + o) % 4) * CHUNK + first, 512), n)

    def rows_at(j, xx, n=64, extra=0):
        return pl.ds(pl.multiple_of(j * TOK + xx * 64 + extra, 32), n)

    near = [plane(0, j)[0] for j in (1, 2, 3)]
    near = [(d - c, tn) for d in near] + [(dp - c, d[1]) for d in (other_zl, right, left)]
    far = [(plane(o, 0)[0] - c + 1, tn) for o in (1, 3)]
    barrier = pltpu.get_barrier_semaphore()
    for peer in near + far:
        pl.semaphore_signal(barrier, inc=1, device_id=peer, device_id_type=MESH)

    @pl.when(c == 1)
    def _():
        pl.semaphore_signal(barrier, inc=1, device_id=other_core, device_id_type=MESH)

    def near_ready():
        @pl.when(c == 0)
        def _():
            pl.semaphore_wait(barrier, 2 * len(near) + 1)
            pl.semaphore_signal(ready, inc=1, device_id=other_core, device_id_type=MESH)

        @pl.when(c == 1)
        def _():
            pl.semaphore_wait(ready, 1)

    def far_ready():
        @pl.when(c == 1)
        def _():
            pl.semaphore_wait(barrier, 2 * len(far))
            pl.semaphore_signal(ready, inc=1, device_id=other_core, device_id_type=MESH)

        @pl.when(c == 0)
        def _():
            pl.semaphore_wait(ready, 1)

    own_rows = rows_at(0, x, 32, zl * 32)
    loads = []
    for k in range(4):
        if k in (1, 2):
            parts = [(o, (k - 1) * 512, 512, to) for o, to in ((1, 0), (3, 512))]
        else:
            parts = [(ORD[k], 0, CHUNK, 0)]
        for o, first, n, to in parts:
            sem = ld.at[k] if to == 0 else ld.at[6 + k]
            loads.append(pltpu.make_async_copy(
                cot_ref.at[:, features(o, first, n)], cot_v.at[k, own_rows, pl.ds(to, n)], sem))
    cot_loads = ((0,), (1, 2), (3, 4), (5,))
    gate_load, up_load, w_load = 6, 7, 8
    loads.append(pltpu.make_async_copy(gate_ref, gate_v, ld.at[4]))
    loads.append(pltpu.make_async_copy(up_ref, up_v, ld.at[5]))

    def quarter_rows(j):
        return pl.ds(pl.multiple_of(((y + j) % 4) * QUARTER, QUARTER), QUARTER)

    def w_rows(j):
        return pl.ds(pl.multiple_of(((y + j) % 2) * 64, 64), QUARTER)

    def w_cols(j, cc):
        return pl.ds(pl.multiple_of((((y + j) % 4) * 2 + cc) * SHARD, SHARD), SHARD)

    loads.append(pltpu.make_async_copy(
        w_ref.at[quarter_rows(0)], w_v.at[3, w_rows(0), w_cols(0, c)], ld.at[6]))
    for load in loads:
        load.start()
    pad = pl.ds(pl.multiple_of((1 - y % 2) * QUARTER, 64), 64)
    for k in range(4):
        w_v[k, pad, :] = jnp.zeros((64, CHUNK), BF16)
    near_ready()

    for k in range(4):
        for n in cot_loads[k]:
            loads[n].wait()
        mine = cot_v.at[k, own_rows]
        start(remote(mine, mine, zl_s.at[k], zl_r.at[k], other_zl))
    partner_rows = rows_at(0, x, 32, (1 - zl) * 32)

    def y_sends(k):
        arrived(cot_v.at[k, partner_rows], zl_r.at[k], zl_s.at[k])
        for j in ((2, 3, 1) if k == 3 else (1, 3, 2)):
            start(remote(cot_v.at[k, rows_at(0, x)], cot_v.at[k, rows_at(back(j), x)],
                         y_s.at[k, j], y_r.at[k, back(j)], plane(0, j)))

    def w_sends():
        for j in (1, 3, 2):
            start(remote(w_ref.at[quarter_rows(j)], w_v.at[3, w_rows(j), w_cols(0, c)],
                         w_s.at[3, back(j)], w_r.at[3, back(j)], plane(0, j)))

    def w_block(k, j, cc):
        if k in (1, 2):
            yy = (y + j) % 4
            col = (k - 1) * 512 + (yy % 2) * 256 + cc * SHARD
            return w_v.at[1 + yy // 2, w_rows(0), pl.ds(pl.multiple_of(col, SHARD), SHARD)]
        return w_v.at[k, w_rows(0), w_cols(j, cc)]

    def w_arrived(k, j):
        if (k, j) == (3, 0):
            loads[w_load].wait()
        else:
            arrived(w_block(k, j, c), w_r.at[k, j], w_s.at[k, j])
        start(remote(w_block(k, j, c), w_block(k, j, c), wc_s.at[k, j], wc_r.at[k, j], other_core))

    def w_own(j):
        w_arrived(3, j)
        for o in (1, 3):
            k = SLOT[back(o)]
            start(remote(w_block(3, j, c), w_block(k, j, c), w_s.at[k, j], w_r.at[k, j],
                         plane(o, 0)))

    def w_near(j):
        for o, passed in ((3, (0, 1)), (1, (2, 3))):
            k = SLOT[back(o)]
            w_arrived(k, j)
            if j in passed:
                start(remote(w_block(k, j, c), w_block(SLOT[2], j, c),
                             w_s.at[SLOT[2], j], w_r.at[SLOT[2], j], plane(o, 0)))

    def w_far():
        for j in range(4):
            w_arrived(SLOT[2], j)

    def w_other(k):
        for j in range(4):
            arrived(w_block(k, j, 1 - c), wc_r.at[k, j], wc_s.at[k, j])

    HOME = (0, 4, 8, 11, 14)

    def home(part):
        if part == 0:
            loads[gate_load].wait()
            loads[up_load].wait()

        def block(f, _):
            cols = pl.ds(pl.multiple_of(f * 128, 128), 128)
            g = gate_v[:, cols].astype(F32)
            u = up_v[:, cols].astype(F32)
            s = jax.nn.sigmoid(g)
            act = g * s
            act_v[:, cols] = act
            fac_v[:, cols] = u * s * (1.0 + g * (1.0 - s))
            hidh[cols, :] = (act * u).T.astype(BF16)
            return 0

        lax.fori_loop(HOME[part], HOME[part + 1], block, 0)

    def hidden_sends():
        for j in (2, 1, 3):
            start(remote(hidh.at[quarter_rows(j)], hidt.at[:, pl.ds(back(j) * TOK, TOK)],
                         h_s.at[j], h_r.at[back(j)], plane(0, j)))
        hidt[:, 0:TOK] = hidh[quarter_rows(0), :]

    def hidden_arrived():
        for j in (1, 3, 2):
            arrived(hidt.at[:, pl.ds(j * TOK, TOK)], h_r.at[j], h_s.at[j])

    def term(k):
        def tile(j, _):
            cols = pl.ds(pl.multiple_of(j * 256, 256), 256)
            part = jnp.dot(hidt[...], cot_v[k, :, cols], preferred_element_type=F32)
            low, high = part[:, :SHARD], part[:, SHARD:]
            pown[j] = jnp.where(c == 0, low, high)
            px_s[k, j] = jnp.where(c == 0, high, low).astype(BF16)
            return 0

        lax.fori_loop(0, 4, tile, 0)
        start(remote(px_s.at[k], px_r.at[k], pc_s.at[k], pc_r.at[k], other_core))

    def term_sends(k):
        arrived(px_r.at[k], pc_r.at[k], pc_s.at[k])
        if k:
            part = pl.ds(2 * (k - 1), 2)
            arrived(pq.at[part], q_r.at[k - 1], q_s.at[k - 1])
        for t in range(4):
            total = pown[t] + px_r[k, t].astype(F32)
            if k and t // 2 == k - 1:
                total = total + pq[t].astype(F32)
            ps[k, t] = total.astype(BF16)
        for n, o in enumerate((1, 3)):
            part = pl.ds(2 * n, 2)
            if k == 0:
                start(remote(ps.at[0, part], pq.at[part], q_s.at[n], q_r.at[n], plane(o, 0)))
            else:
                start(remote(ps.at[k, part], pz.at[n, pl.ds(2 * (k - 1), 2)],
                             p_s.at[k, n], p_r.at[k, n], plane(o, 0)))

    def last_part(block, j):
        cols = pl.ds(pl.multiple_of(((y + j) % 4) * 256, 256), 256)
        return jnp.dot(hidt[:, pl.ds(block * TOK, TOK)], cot_v[3, pl.ds(block * TOK, TOK), cols],
                       preferred_element_type=F32)

    def last_add(block):
        first = ("ladd",) not in done_once
        done_once.add(("ladd",))

        def tile(j, _):
            part = last_part(block, j)
            pacc[j] = part if first else pacc[j] + part
            return 0

        lax.fori_loop(0, 4, tile, 0)

    def last_terms():
        for j in (2, 1, 3, 0):
            part = pacc[j] + last_part(0, j)
            low, high = part[:, :SHARD], part[:, SHARD:]
            px_s[3, j] = jnp.where(c == 0, high, low).astype(BF16)
            start(remote(px_s.at[3, j], px_r.at[3, j], l_s.at[j], l_r.at[j], other_core))
            pown[j] = jnp.where(c == 0, low, high)

    def last_sends():
        for k in (1, 2):
            for n in range(2):
                arrived(pz.at[n, pl.ds(2 * (k - 1), 2)], p_r.at[k, n], p_s.at[k, n])
        for j in (2, 1, 3, 0):
            arrived(px_r.at[3, j], l_r.at[j], l_s.at[j])
            yy = (y + j) % 4
            total = pown[j] + px_r[3, j].astype(F32) + (pz[0, yy].astype(F32) + pz[1, yy].astype(F32))
            if j:
                ps[3, j] = total.astype(BF16)
                start(remote(ps.at[3, j], py.at[back(j)], py_s.at[j], py_r.at[back(j)], plane(0, j)))
            else:
                gp_v[quarter_rows(0), :] = total * unscale

    def grad_part(k, j):
        rows = pl.ds(j * TOK, TOK) if isinstance(j, int) else pl.ds(pl.multiple_of(j * TOK, TOK), TOK)
        return lax.dot_general(cot_v[k, rows, :], w_v[k], (((1,), (1,)), ((), ())),
                               preferred_element_type=F32)

    def grad_add(k):
        first = ("gadd",) not in done_once
        done_once.add(("gadd",))

        def tile(j, _):
            part = grad_part(k, j)
            hg_acc[j] = part if first else hg_acc[j] + part
            return 0

        lax.fori_loop(0, 4, tile, 0)

    def grad_sends(j):
        hg_s[j] = (hg_acc[j] + grad_part(3, j)).astype(BF16)
        if j == 0:
            copy = pltpu.make_async_copy(hg_s.at[0], hg_r.at[y], g_r.at[y])
            copy.start()
        else:
            start(remote(hg_s.at[j], hg_r.at[y], g_s.at[j], g_r.at[y], plane(0, j)))

    def own(k, j):
        if j:
            arrived(cot_v.at[k, rows_at(j, x)], y_r.at[k, j], y_s.at[k, j])
        mine = cot_v.at[k, rows_at(j, x)]
        start(remote(mine, mine, xr_s.at[k, j], fl_r.at[k, j], right))
        start(remote(mine, mine, xl_s.at[k, j], fr_r.at[k, j], left))

    def forward(k, j):
        from_left = cot_v.at[k, rows_at(j, (x + 3) % 4)]
        from_right = cot_v.at[k, rows_at(j, (x + 1) % 4)]
        arrived(from_left, fl_r.at[k, j], xr_s.at[k, j])
        arrived(from_right, fr_r.at[k, j], xl_s.at[k, j])
        block, device = (from_left, right) if j in RIGHT else (from_right, left)
        start(remote(block, block, xf_s.at[k, j], xf_r.at[k, j], device))

    def done(k, j):
        arrived(cot_v.at[k, rows_at(j, (x + 2) % 4)], xf_r.at[k, j], xf_s.at[k, j])

    stores = []

    def result(r, _):
        rows = pl.ds(pl.multiple_of(r * 32, 32), 32)
        p = [hg_r[q, rows, :].astype(F32) for q in range(4)]
        grad = jnp.concatenate(
            [p[0][:, :384], p[0][:, 384:] + p[1][:, :128], p[1][:, 128:],
             p[2][:, :384], p[2][:, 384:] + p[3][:, :128], p[3][:, 128:]], axis=1)
        ug_v[rows, :] = (grad * act_v[rows, :]).astype(BF16)
        gg_v[rows, :] = (grad * fac_v[rows, :]).astype(BF16)
        return 0

    def grad_results():
        for yy in range(4):
            arrived(hg_r.at[yy], g_r.at[yy], g_s.at[0])
        for half in range(2):
            lax.fori_loop(half * 4, half * 4 + 4, result, 0)
            rows = pl.ds(half * 128, 128)
            for n, (src, dst) in enumerate(((ug_v, ug_ref), (gg_v, gg_ref))):
                stores.append(pltpu.make_async_copy(
                    src.at[rows], dst.at[rows], out_s.at[half * 2 + n]))
                stores[-1].start()

    def term_results():
        for j in (0, 1, 3, 2):
            if j:
                arrived(py.at[j], py_r.at[j], py_s.at[j])
                gp_v[quarter_rows(j), :] = py[j].astype(F32) * unscale
            stores.append(pltpu.make_async_copy(
                gp_v.at[quarter_rows(j)], gp_ref.at[quarter_rows(j)], out_s.at[4 + j]))
            stores[-1].start()

    def b_rows(j, n, first=0, size=64):
        return rows_at(j, (x + (0, 3, 1, 2)[n]) % 4, size, first)

    def b_ref(*rows):
        return cot_v.at[ALONG_X, b_rows(*rows)]

    def b_own():
        arrived(cot_v.at[ALONG_X, partner_rows], zl_r.at[ALONG_X], zl_s.at[ALONG_X])
        mine = b_ref(0, 0)
        start(remote(mine, mine, xr_s.at[ALONG_X, 0], fl_r.at[ALONG_X, 0], right))
        start(remote(mine, mine, xl_s.at[ALONG_X, 0], fr_r.at[ALONG_X, 0], left))

    def b_forward():
        arrived(b_ref(0, 1), fl_r.at[ALONG_X, 0], xr_s.at[ALONG_X, 0])
        arrived(b_ref(0, 2), fr_r.at[ALONG_X, 0], xl_s.at[ALONG_X, 0])
        for n, device in ((1, right), (2, left)):
            half = b_ref(0, n, 32 * (n - 1), 32)
            start(remote(half, half, xf_s.at[ALONG_X, n], xf_r.at[ALONG_X, n], device))

    def b_y(n):
        if n == 3:
            for m in (1, 2):
                arrived(b_ref(0, 3, 32 * (m - 1), 32), xf_r.at[ALONG_X, m], xf_s.at[ALONG_X, m])
        for j in (1, 3, 2):
            start(remote(b_ref(0, n), b_ref(back(j), n), by_s.at[n, j], by_r.at[n, back(j)],
                         plane(0, j)))

    def b_done():
        for n in range(4):
            for j in (1, 3, 2):
                arrived(b_ref(j, n), by_r.at[n, j], by_s.at[n, j])

    steps = dict(
        bown=b_own, bfwd=b_forward, by=b_y, bdone=b_done,
        ysend=y_sends, own=own, fwd=forward, done=done, wsend=w_sends, farr=far_ready, wown=w_own,
        wnear=w_near, wfar=w_far, woth=w_other, home=home, hsend=hidden_sends,
        harr=hidden_arrived, term=term, tsend=term_sends, gadd=grad_add, ladd=last_add,
        gsend=grad_sends, lterms=last_terms, lsends=last_sends, gres=grad_results,
        pres=term_results,
    )
    for name, *place in ORDER:
        steps[name](*place)
    for copy in sent:
        copy.wait_send()
    for store in stores:
        store.wait()


def grads(gate_pre, up_pre, cotangent, w_prev):
    def dma(*shape):
        return pltpu.SemaphoreType.DMA(shape)

    any_spec = pl.BlockSpec(memory_space=pl.ANY)
    scratch = [
        pltpu.VMEM((TOK, HID), BF16),
        pltpu.VMEM((TOK, HID), BF16),
        pltpu.VMEM((TOK, HID), F32),
        pltpu.VMEM((TOK, HID), F32),
        pltpu.VMEM((HID, TOK), BF16),
        pltpu.VMEM((QUARTER, 4 * TOK), BF16),
        pltpu.VMEM((4, 4 * TOK, CHUNK), BF16),
        pltpu.VMEM((4, WIDE, CHUNK), BF16),
        pltpu.VMEM((4, 4, QUARTER, SHARD), BF16),
        pltpu.VMEM((4, 4, QUARTER, SHARD), BF16),
        pltpu.VMEM((4, QUARTER, SHARD), F32),
        pltpu.VMEM((4, QUARTER, 256), F32),
        pltpu.VMEM((4, 4, QUARTER, SHARD), BF16),
        pltpu.VMEM((4, QUARTER, SHARD), BF16),
        pltpu.VMEM((2, 4, QUARTER, SHARD), BF16),
        pltpu.VMEM((4, QUARTER, SHARD), BF16),
        pltpu.VMEM((4, TOK, WIDE), F32),
        pltpu.VMEM((4, TOK, WIDE), BF16),
        pltpu.VMEM((4, TOK, WIDE), BF16),
        pltpu.VMEM((TOK, HID), BF16),
        pltpu.VMEM((TOK, HID), BF16),
        pltpu.VMEM((HID, SHARD), F32),
        dma(10), dma(4), dma(4), dma(4, 4), dma(4, 4),
        dma(4, 4), dma(4, 4), dma(4, 4), dma(4, 4), dma(4, 4), dma(4, 4),
        dma(4, 4), dma(4, 4), dma(4, 4), dma(4, 4),
        dma(4), dma(4), dma(4), dma(4),
        dma(4), dma(4), dma(2), dma(2), dma(3, 2), dma(3, 2), dma(4), dma(4),
        dma(4), dma(4), dma(4, 4), dma(4, 4), dma(8),
        pltpu.SemaphoreType.REGULAR,
    ]
    return pl.pallas_call(
        kernel,
        out_shape=(
            jax.ShapeDtypeStruct((TOK, HID), BF16),
            jax.ShapeDtypeStruct((TOK, HID), BF16),
            jax.ShapeDtypeStruct((HID, SHARD), F32),
        ),
        in_specs=[any_spec] * 4,
        out_specs=(any_spec,) * 3,
        scratch_shapes=scratch,
        compiler_params=pltpu.CompilerParams(
            collective_id=0, has_side_effects=True, vmem_limit_bytes=62 * 2**20
        ),
        cost_estimate=pl.CostEstimate(
            flops=4 * TOK * HID * 4096, bytes_accessed=8 * 2**20, transcendentals=TOK * HID
        ),
    )(gate_pre, up_pre, cotangent, w_prev)


def finish_kernel(
    gg, ug, gp, param, grad, one, two, gg_out, ug_out, gp_out, param_out, one_out, two_out, step_out
):
    gg_out[...] = gg[...]
    ug_out[...] = ug[...]
    gp_out[...] = gp[...]
    g = grad[...]
    moment_one_f = beta_first * one[...].astype(F32) + (1.0 - beta_first) * g
    moment_two_f = beta_second * two[...].astype(F32) + (1.0 - beta_second) * g * g
    first_fix = 1.0 - beta_first**STEP
    second_fix = 1.0 - beta_second**STEP
    adam_step = (
        moment_one_f / first_fix / (jnp.sqrt(moment_two_f / second_fix) + epsilon)
        + decay_rate * param[...]
    )
    param_out[...] = param[...] - learn_rate * adam_step
    one_out[...] = moment_one_f.astype(BF16)
    two_out[...] = moment_two_f.astype(BF16)
    step_out[...] = adam_step


def finish(gate_grad, up_grad, grad_prev, param_next, grad_next, moment_one, moment_two):
    parts = 2
    tokens = pl.BlockSpec((TOK // parts, HID), lambda i: (i, 0))
    part = pl.BlockSpec((HID // parts, SHARD), lambda i: (i, 0))

    def like(*arrays):
        return tuple(jax.ShapeDtypeStruct(a.shape, a.dtype) for a in arrays)

    return pl.pallas_call(
        finish_kernel,
        grid=(parts,),
        out_shape=like(gate_grad, up_grad, grad_prev, param_next, moment_one, moment_two, param_next),
        in_specs=[tokens] * 2 + [part] * 5,
        out_specs=(tokens,) * 2 + (part,) * 5,
        cost_estimate=pl.CostEstimate(
            flops=20 * HID * SHARD, bytes_accessed=12 * 2**20, transcendentals=2 * HID * SHARD
        ),
    )(gate_grad, up_grad, grad_prev, param_next, grad_next, moment_one, moment_two)


def body(gate_pre, up_pre, cotangent, w_prev, param_next, grad_next, moment_one, moment_two):
    partial = grads(gate_pre, up_pre, cotangent, w_prev)
    return finish(*partial, param_next, grad_next, moment_one, moment_two)


def solution(mesh):
    in_specs = (
        P("dp", "tensor"),
        P("dp", "tensor"),
        P(("dp", "tensor"), None),
        P("tensor", "dp"),
        P("tensor", "dp"),
        P("tensor", "dp"),
        P("tensor", "dp"),
        P("tensor", "dp"),
    )
    out_specs = (
        P("dp", "tensor"),
        P("dp", "tensor"),
        P("tensor", "dp"),
        P("tensor", "dp"),
        P("tensor", "dp"),
        P("tensor", "dp"),
        P("tensor", "dp"),
    )
    return jax.shard_map(body, mesh=mesh, in_specs=in_specs, out_specs=out_specs, check_vma=False)
```
